32 devices in a mesh: group: 2 (over x), row: 16 (over z, y, core), feat: 1.
Axes of the slice: x: 2, y: 2, z: 4, core: 2. Of those that a mesh axis runs over, the one named last changes fastest.
Arguments:
- cells: bfloat16 [1024, 256, 128], P(('group', 'row'), 'feat'), parts along dimension 0, may hold values from -6 to 6
- is_context: int32 [1024], P(('group', 'row')), parts along dimension 0, may hold values from 0 to 1, as said below
- labels: int32 [1024], P(('group', 'row', 'feat')), parts along dimension 0, may hold values from 0 to 9
- inducing: bfloat16 [96, 128], replicated, may hold values from -6 to 6
- induce_query: bfloat16 [128, 128], replicated, may hold values from -1.5 to 1.5
- column_kvo: bfloat16 [3, 128, 128], replicated, may hold values from -0.5 to 0.5
- cell_qkvo: bfloat16 [4, 128, 128], replicated, may hold values from -0.5 to 0.5
- class_tokens: bfloat16 [4, 128], replicated, may hold values from -6 to 6
- class_query: bfloat16 [128, 128], replicated, may hold values from -1.5 to 1.5
- row_kvo: bfloat16 [3, 128, 128], replicated, may hold values from -0.5 to 0.5
- label_table: bfloat16 [10, 512], replicated, may hold values from -6 to 6
- icl_query: bfloat16 [512, 512], replicated, may hold values from -0.75 to 0.75
- icl_kvo: bfloat16 [3, 512, 512], replicated, may hold values from -0.25 to 0.25
Outputs:
- row_outputs: bfloat16 [1024, 512], P(('group', 'row', 'feat')), parts along dimension 0
The draws below stay inside these ranges and needn't reach their ends.
There are 2 independent parts, one for each index of `group`. The reference program is written for one: setup_inputs(seed, part) draws one part's arguments, and reference() takes and returns one part's arrays. A program takes and returns all parts, laid end to end along the dimension named above; an argument that names none is the same for every part. Nothing has to cross between parts.
Inputs may be any that keep to these rules, and one draw needn't show every extreme that they name: `is_context`: 1 marks a labelled context row, 0 a query row; every window holds context rows.
All inputs are finite; a program needn't handle non-finite values.
Results may differ from the reference program's by a relative error of at most 0.017.
Values may be sent and summed in bfloat16 or wider, within the bound.
A program may use at most 128 MiB of HBM per device.

```python
import math
import jax
import jax.numpy as jnp
from jax import lax

CELL_WIDTH = 128
F = 256
M = 96
HEADS = 4
ROW_HEADS = 8
CLS = 4
C = 10
R_DEV = 32
WINDOW_ROWS = 512
DH = 32
DF = 16
D3 = 512
DR = 128


def draw_is_context(key, part):
    start_key = jax.random.fold_in(key, 11)
    flag_key = jax.random.fold_in(key, 23)
    run_length = max(2 * R_DEV, WINDOW_ROWS // 4)
    run_start = jax.random.randint(start_key, (), 0, WINDOW_ROWS - run_length + 1, dtype=jnp.int32)
    positions = jnp.arange(WINDOW_ROWS, dtype=jnp.int32)
    inside = (positions >= run_start) & (positions < run_start + run_length)
    scattered = jax.random.randint(flag_key, (WINDOW_ROWS,), 0, 2, dtype=jnp.int32)
    return jnp.where(inside, jnp.ones_like(scattered), scattered).astype(jnp.int32)


def draw_class_tokens(key, part):
    values = jnp.clip(jax.random.normal(jax.random.fold_in(key, 37), (CLS, CELL_WIDTH), jnp.float32), -6.0, 6.0)
    return values.astype(jnp.bfloat16)


def with_ends(result, own_key, least, largest):
    spot = [jax.random.randint(jax.random.fold_in(own_key, axis), (), 0, length) for axis, length in enumerate(result.shape)]
    main_axis = result.shape.index(max(result.shape))
    next_to = spot[:main_axis] + [(spot[main_axis] + 1) % result.shape[main_axis]] + spot[main_axis + 1:]
    return result.at[tuple(spot)].set(least).at[tuple(next_to)].set(largest)


def block_scale(rng, extent, pieces, least, top_value):
    gain, own = 1.0, jax.random.fold_in(rng, 6)
    for position, shards_of in pieces:
        heights = jnp.exp(jax.random.uniform(jax.random.fold_in(own, position), (shards_of,), jnp.float32, least / len(pieces), top_value / len(pieces)))
        gain = gain * jnp.repeat(heights, extent[position] // shards_of).reshape([-1 if axis == position else 1 for axis in range(len(extent))])
    return gain


def noise(key, extent, scale, bound, split=(), kind=jnp.bfloat16):
    gain = block_scale(key, extent, split, -0.22, 0.18) if split else 1.0
    result = jax.random.normal(key, extent, jnp.float32) * scale * gain
    return jnp.minimum(jnp.maximum(result, -bound), bound).astype(kind)


def setup_inputs(seed: int = 0, part: int = 0) -> dict:
    key_of = jax.random.split(jax.random.key(seed), 14)
    part_splits = jax.random.split(jax.random.fold_in(key_of[13], part), 14)
    cells = noise(part_splits[0], (WINDOW_ROWS, F, CELL_WIDTH), 1.0, 6.0, ((0, 16),))
    is_context = draw_is_context(jax.random.fold_in(jax.random.fold_in(key_of[13], part), 71), part)
    labels = with_ends(jax.random.randint(part_splits[2], (WINDOW_ROWS,), 0, C), jax.random.fold_in(part_splits[2], 1), 0, C - 1).astype(jnp.int32)
    inducing = noise(key_of[3], (M, CELL_WIDTH), 1.0, 6.0)
    induce_query = noise(key_of[4], (CELL_WIDTH, CELL_WIDTH), (CELL_WIDTH // 9) ** -0.5, 1.5)
    column_kvo = noise(key_of[5], (3, CELL_WIDTH, CELL_WIDTH), CELL_WIDTH ** -0.5, 0.5)
    cell_qkvo = noise(key_of[6], (4, CELL_WIDTH, CELL_WIDTH), CELL_WIDTH ** -0.5, 0.5)
    class_tokens = draw_class_tokens(jax.random.fold_in(key_of[13], 71), part)
    class_query = noise(key_of[8], (CELL_WIDTH, CELL_WIDTH), (CELL_WIDTH // 9) ** -0.5, 1.5)
    row_kvo = noise(key_of[9], (3, CELL_WIDTH, CELL_WIDTH), CELL_WIDTH ** -0.5, 0.5)
    label_table = noise(key_of[10], (C, D3), 1.0, 6.0)
    icl_query = noise(key_of[11], (D3, D3), (D3 // 9) ** -0.5, 0.75)
    icl_kvo = noise(key_of[12], (3, D3, D3), D3 ** -0.5, 0.25)
    return {"cells": cells, "is_context": is_context, "labels": labels, "inducing": inducing, "induce_query": induce_query, "column_kvo": column_kvo, "cell_qkvo": cell_qkvo, "class_tokens": class_tokens, "class_query": class_query, "row_kvo": row_kvo, "label_table": label_table, "icl_query": icl_query, "icl_kvo": icl_kvo}


epsilon = 1e-06

def narrow_precision(value):
    return lax.optimization_barrier(value.astype(jnp.bfloat16))

def promote_precision(value):
    return value.astype(jnp.float32)

def reference(cells, is_context, labels, inducing, induce_query, column_kvo, cell_qkvo, class_tokens, class_query, row_kvo, label_table, icl_query, icl_kvo):
    context_rows = (is_context == 1).astype(jnp.float32)
    scale_factor = 1.0 / math.sqrt(DH)
    feat_scaling = 1.0 / math.sqrt(DF)
    inducing_query = promote_precision(narrow_precision(jnp.dot(inducing, induce_query, preferred_element_type=jnp.float32))).reshape(M, HEADS, DH)
    cls_query = promote_precision(narrow_precision(jnp.dot(class_tokens, class_query, preferred_element_type=jnp.float32))).reshape(CLS, ROW_HEADS, DF)
    cls_keys = promote_precision(narrow_precision(jnp.dot(class_tokens, row_kvo[0], preferred_element_type=jnp.float32))).reshape(CLS, ROW_HEADS, DF)
    cls_values = promote_precision(narrow_precision(jnp.dot(class_tokens, row_kvo[1], preferred_element_type=jnp.float32))).reshape(CLS, ROW_HEADS, DF)
    cls_weight = jnp.exp(jnp.einsum('chd,khd->chk', cls_query, cls_keys) * feat_scaling)
    cls_denom = lax.optimization_barrier(jnp.sum(cls_weight, axis=-1))
    cls_numer = jnp.einsum('chk,khd->chd', promote_precision(narrow_precision(cls_weight)), cls_values)

    def feature_step(running, column):
        column_keys = promote_precision(narrow_precision(jnp.dot(column, column_kvo[0], preferred_element_type=jnp.float32))).reshape(WINDOW_ROWS, HEADS, DH)
        column_values = promote_precision(narrow_precision(jnp.dot(column, column_kvo[1], preferred_element_type=jnp.float32))).reshape(WINDOW_ROWS, HEADS, DH)
        column_weight = jnp.exp(jnp.einsum('ysu,jsu->syj', inducing_query, column_keys) * scale_factor) * context_rows[None, None, :]
        col_denom = lax.optimization_barrier(jnp.sum(column_weight, axis=-1))
        column_numerator = jnp.einsum('bka,abu->kbu', promote_precision(narrow_precision(column_weight)), column_values)
        col_mix = narrow_precision(column_numerator / jnp.transpose(col_denom)[:, :, None]).reshape(M, CELL_WIDTH)
        summary = narrow_precision(promote_precision(inducing) + jnp.dot(col_mix, column_kvo[2], preferred_element_type=jnp.float32))
        cell_query_rows = promote_precision(narrow_precision(jnp.dot(column, cell_qkvo[0], preferred_element_type=jnp.float32))).reshape(WINDOW_ROWS, HEADS, DH)
        summary_keys = promote_precision(narrow_precision(jnp.dot(summary, cell_qkvo[1], preferred_element_type=jnp.float32))).reshape(M, HEADS, DH)
        summary_values = promote_precision(narrow_precision(jnp.dot(summary, cell_qkvo[2], preferred_element_type=jnp.float32))).reshape(M, HEADS, DH)
        unscaled_weight = jnp.exp(jnp.einsum('gie,jie->ijg', cell_query_rows, summary_keys) * scale_factor)
        cell_weight_matrix = promote_precision(narrow_precision(unscaled_weight / lax.optimization_barrier(jnp.sum(unscaled_weight, axis=1, keepdims=True))))
        cell_blend = narrow_precision(jnp.einsum('agb,gav->bav', cell_weight_matrix, summary_values)).reshape(WINDOW_ROWS, CELL_WIDTH)
        column_out = promote_precision(column) + jnp.dot(cell_blend, cell_qkvo[3], preferred_element_type=jnp.float32)
        embedded = narrow_precision(column_out * lax.rsqrt(lax.optimization_barrier(jnp.mean(column_out * column_out, axis=-1, keepdims=True)) + epsilon))
        cell_keys = promote_precision(narrow_precision(jnp.dot(embedded, row_kvo[0], preferred_element_type=jnp.float32))).reshape(WINDOW_ROWS, ROW_HEADS, DF)
        cell_values = promote_precision(narrow_precision(jnp.dot(embedded, row_kvo[1], preferred_element_type=jnp.float32))).reshape(WINDOW_ROWS, ROW_HEADS, DF)
        row_weight = jnp.exp(jnp.einsum('chd,rhd->rch', cls_query, cell_keys) * feat_scaling)
        row_numer, row_denom = running
        row_numer = row_numer + jnp.einsum('rch,rhd->rchd', promote_precision(narrow_precision(row_weight)), cell_values)
        return ((row_numer, row_denom + row_weight), None)
    start_zero = (jnp.zeros((WINDOW_ROWS, CLS, ROW_HEADS, DF), jnp.float32), jnp.zeros((WINDOW_ROWS, CLS, ROW_HEADS), jnp.float32))
    (row_numer, row_denom), _ = lax.scan(feature_step, start_zero, jnp.transpose(cells, (1, 0, 2)))
    row_numer = row_numer + cls_numer[None]
    row_denom = row_denom + cls_denom[None]
    row_mix = narrow_precision(row_numer / row_denom[..., None]).reshape(WINDOW_ROWS * CLS, CELL_WIDTH)
    row_embed = narrow_precision(promote_precision(class_tokens)[None] + jnp.dot(row_mix, row_kvo[2], preferred_element_type=jnp.float32).reshape(WINDOW_ROWS, CLS, CELL_WIDTH)).reshape(WINDOW_ROWS, D3)
    one_hot = (labels[:, None] == jnp.arange(C, dtype=jnp.int32)[None, :]).astype(jnp.bfloat16)
    label_vec = jnp.dot(one_hot, label_table, preferred_element_type=jnp.float32)
    icl_input = narrow_precision(promote_precision(row_embed) + context_rows[:, None] * label_vec)
    query_rows = promote_precision(narrow_precision(jnp.dot(row_embed, icl_query, preferred_element_type=jnp.float32))).reshape(WINDOW_ROWS, HEADS, DR)
    key_rows = promote_precision(narrow_precision(jnp.dot(icl_input, icl_kvo[0], preferred_element_type=jnp.float32))).reshape(WINDOW_ROWS, HEADS, DR)
    value_rows = promote_precision(narrow_precision(jnp.dot(icl_input, icl_kvo[1], preferred_element_type=jnp.float32))).reshape(WINDOW_ROWS, HEADS, DR)
    row_scaling = 1.0 / math.sqrt(DR)
    query_block = math.gcd(WINDOW_ROWS, 512)

    def block_attend(queries):
        icl_weight = jnp.exp(jnp.einsum('qhd,khd->qhk', queries, key_rows) * row_scaling) * context_rows[None, None, :]
        numer = jnp.einsum('qhk,khd->qhd', promote_precision(narrow_precision(icl_weight)), value_rows)
        return narrow_precision(numer / lax.optimization_barrier(jnp.sum(icl_weight, axis=-1))[..., None])
    icl_mix = lax.map(block_attend, query_rows.reshape(WINDOW_ROWS // query_block, query_block, HEADS, DR)).reshape(WINDOW_ROWS, D3)
    return (promote_precision(row_embed) + jnp.dot(icl_mix, icl_kvo[2], preferred_element_type=jnp.float32)).astype(jnp.bfloat16)
```

```python
import math

import jax
import jax.numpy as jnp
from jax import lax
from jax.experimental import pallas as pl
from jax.experimental.pallas import tpu as pltpu
from jax.sharding import PartitionSpec as P

HEADS = 4
ROW_HEADS = 8
EPSILON = 1e-06
LOG2E = math.log2(math.e)

F32 = jnp.float32
BF16 = jnp.bfloat16


def mm(a, b):
    return jnp.dot(a, b, preferred_element_type=F32)


def mm_nt(a, b):
    return lax.dot_general(a, b, (((1,), (1,)), ((), ())), preferred_element_type=F32)


def flip(w):
    return w.astype(F32).T.astype(BF16)


def head_rows(shape, row_block, lane_block, n):
    rows = lax.broadcasted_iota(jnp.int32, shape, 0) // row_block
    lanes = lax.broadcasted_iota(jnp.int32, shape, 1) // lane_block
    return lax.rem(rows, n) == lax.rem(lanes, n)


def row_queries(ct, class_query):
    n_class, width = ct.shape
    rq = mm(ct, class_query).astype(BF16).astype(F32)
    shape = (n_class * ROW_HEADS, width)
    rq = jnp.broadcast_to(rq[:, None, :], (n_class, ROW_HEADS, width)).reshape(shape)
    return jnp.where(head_rows(shape, 1, width // ROW_HEADS, ROW_HEADS), rq, 0.0)


def prepare(ind, iq_w, ckvo, cqkvo, ct, cq_w, rkvo, wcol, wrow, wt):
    n_ind, width = ind.shape
    iq = mm(ind[...], iq_w[...]).astype(BF16).astype(F32)
    iq = jnp.concatenate([iq] * HEADS, axis=0)
    iq = jnp.where(head_rows(iq.shape, n_ind, width // HEADS, HEADS), iq, 0.0).astype(BF16)
    scale = LOG2E / math.sqrt(width // HEADS)
    wcol[...] = (mm_nt(iq, ckvo[0]) * scale).astype(BF16)
    rq = row_queries(ct[...], cq_w[...]).astype(BF16)
    row_scale = LOG2E / math.sqrt(width // ROW_HEADS)
    wrow[...] = (mm_nt(rq, rkvo[0]) * row_scale).astype(BF16)
    wt[0] = flip(cqkvo[0])
    wt[1] = flip(cqkvo[2])
    wt[2] = flip(cqkvo[3])
    wt[3] = flip(rkvo[1])


def feature(x, maskb, ind, ckvo, cqkvo, wcol, wrow, wt):
    n_ind, width = ind.shape
    head = width // HEADS
    xt = x.T
    weight = jnp.exp2(mm(wcol[...], xt)).astype(BF16)
    values = mm(x, ckvo[1]).astype(BF16) * maskb
    numer = mm(weight, jnp.concatenate([values, maskb], axis=1))
    ratio = numer[:, :width] / numer[:, width:]
    lane_head = lax.broadcasted_iota(jnp.int32, (n_ind, width), 1) // head
    col_mix = ratio[:n_ind]
    for h in range(1, HEADS):
        col_mix = jnp.where(lane_head == h, ratio[h * n_ind : (h + 1) * n_ind], col_mix)
    summary = (ind[...].astype(F32) + mm(col_mix.astype(BF16), ckvo[2])).astype(BF16)
    scale = LOG2E / math.sqrt(head)
    keys = mm(summary, cqkvo[1]) * scale
    keys = jnp.concatenate([keys] * HEADS, axis=0)
    keys = jnp.where(head_rows(keys.shape, n_ind, head, HEADS), keys, 0.0).astype(BF16)
    sum_values = mm_nt(wt[1], jnp.concatenate([summary] * HEADS, axis=0))
    sum_values = jnp.where(head_rows(sum_values.shape, head, n_ind, HEADS), sum_values, 0.0)
    sum_values = sum_values.astype(BF16)
    query = mm(wt[0], xt).astype(BF16)
    cell = jnp.exp2(mm(keys, query))
    blocks = []
    for h in range(HEADS):
        part = cell[h * n_ind : (h + 1) * n_ind]
        blocks.append((part * (1.0 / jnp.sum(part, axis=0, keepdims=True))).astype(BF16))
    cell = jnp.concatenate(blocks, axis=0)
    mix = mm(sum_values, cell).astype(BF16)
    out = xt.astype(F32) + mm(wt[2], mix)
    inv = lax.rsqrt(jnp.mean(out * out, axis=0, keepdims=True) + EPSILON)
    embedded = (out * inv).astype(BF16)
    row_weight = jnp.exp2(mm(wrow[...], embedded))
    row_values = mm(wt[3], embedded).astype(BF16).astype(F32)
    return row_weight, row_values


def accumulate(terms, acc, den, n_class):
    width = terms[0][1].shape[0]
    total = terms[0][0]
    for weight, _ in terms[1:]:
        total = total + weight
    den[...] += total
    for c in range(n_class):
        add = None
        for weight, values in terms:
            w = weight[c * ROW_HEADS : (c + 1) * ROW_HEADS].astype(BF16).astype(F32)
            n = w.shape[1]
            w = jnp.broadcast_to(w[:, None, :], (ROW_HEADS, width // ROW_HEADS, n)).reshape(width, n)
            add = w * values if add is None else add + w * values
        acc[c] += add


def finish(acc, den, out_ref):
    n_class, width, _ = acc.shape
    for c in range(n_class):
        out_ref[:, c * width : (c + 1) * width] = acc[c].T.astype(BF16)
    d = den[...]
    pad = jnp.zeros((width - d.shape[0], d.shape[1]), F32)
    out_ref[:, n_class * width :] = jnp.concatenate([d, pad], axis=0).T.astype(BF16)


def column_kernel(x_ref, maskb, ind, iq_w, ckvo, cqkvo, ct, cq_w, rkvo, out_ref, wcol, wrow, wt, acc, den):
    step = pl.program_id(0)

    @pl.when(step == 0)
    def _():
        prepare(ind, iq_w, ckvo, cqkvo, ct, cq_w, rkvo, wcol, wrow, wt)
        acc[...] = jnp.zeros_like(acc)
        den[...] = jnp.zeros_like(den)

    n_src, n_feat, n_rows, width = x_ref.shape
    terms = []
    for f in range(n_feat):
        x = x_ref[:, f].reshape(n_src * n_rows, width)
        terms.append(feature(x, maskb[...], ind, ckvo, cqkvo, wcol, wrow, wt))
    accumulate(terms, acc, den, ct.shape[0])

    @pl.when(step == pl.num_programs(0) - 1)
    def _():
        finish(acc, den, out_ref)


def embed_rows(total, ct, cq_w, rkvo, context, labels, table):
    n_class, width = ct.shape
    n_rows = total.shape[0]
    queries = row_queries(ct[...], cq_w[...])
    keys = mm(ct[...], rkvo[0]).astype(BF16).astype(F32)
    values = mm(ct[...], rkvo[1]).astype(BF16).astype(F32)
    scale = LOG2E / math.sqrt(width // ROW_HEADS)
    cls_den = jnp.zeros((n_class * ROW_HEADS, 1), F32)
    cls_num = jnp.zeros((n_class * ROW_HEADS, width), F32)
    for t in range(n_class):
        w = jnp.exp2(jnp.sum(queries * keys[t : t + 1], axis=1, keepdims=True) * scale)
        cls_den = cls_den + w
        cls_num = cls_num + w.astype(BF16).astype(F32) * values[t : t + 1]
    shape = cls_num.shape
    own = head_rows(shape, 1, width // ROW_HEADS, ROW_HEADS)
    cls_num = jnp.where(own, cls_num, 0.0)
    cls_den = jnp.where(own, jnp.broadcast_to(cls_den, shape), 0.0)
    lane_head = lax.broadcasted_iota(jnp.int32, (n_rows, width), 1) // (width // ROW_HEADS)
    embeds = []
    for c in range(n_class):
        rows = slice(c * ROW_HEADS, (c + 1) * ROW_HEADS)
        numer = total[:, c * width : (c + 1) * width] + jnp.sum(cls_num[rows], axis=0, keepdims=True)
        denom = jnp.zeros((n_rows, width), F32)
        for h in range(ROW_HEADS):
            at = n_class * width + c * ROW_HEADS + h
            denom = jnp.where(lane_head == h, total[:, at : at + 1], denom)
        denom = denom + jnp.sum(cls_den[rows], axis=0, keepdims=True)
        mix = (numer / denom).astype(BF16)
        embeds.append((ct[c : c + 1].astype(F32) + mm(mix, rkvo[2])).astype(BF16))
    row_embed = jnp.concatenate(embeds, axis=1)
    label_vec = jnp.zeros((n_rows, n_class * width), F32)
    for k in range(table.shape[0]):
        label_vec = jnp.where(labels == k, table[k : k + 1].astype(F32), label_vec)
    icl_input = (row_embed.astype(F32) + context * label_vec).astype(BF16)
    return row_embed, icl_input


def embed_kernel(parts, ct, cq_w, rkvo, context, labels, table, embed_ref, input_ref):
    total = parts[0].astype(F32)
    for i in range(1, parts.shape[0]):
        total = total + parts[i].astype(F32)
    embed, icl = embed_rows(total, ct, cq_w, rkvo, context[...], labels[...], table)
    embed_ref[...] = embed
    input_ref[...] = icl


def in_context(embed, inputs, mask, icl_q, icl_kvo):
    width = embed.shape[1]
    head = width // HEADS
    query = mm(embed, icl_q[...]).astype(BF16)
    keys = mm(inputs, icl_kvo[0]).astype(BF16)
    values = mm(inputs, icl_kvo[1]).astype(BF16)
    scale = LOG2E / math.sqrt(head)
    mixes = []
    for h in range(HEADS):
        lanes = slice(h * head, (h + 1) * head)
        weight = jnp.exp2(mm_nt(query[:, lanes], keys[:, lanes]) * scale) * mask
        denom = jnp.sum(weight, axis=1, keepdims=True)
        mixes.append((mm(weight.astype(BF16), values[:, lanes]) / denom).astype(BF16))
    mix = jnp.concatenate(mixes, axis=1)
    return (embed.astype(F32) + mm(mix, icl_kvo[2])).astype(BF16)


def context_kernel(embed, inputs, mask, icl_q, icl_kvo, out_ref):
    out_ref[...] = in_context(embed[...], inputs[...], mask[...], icl_q, icl_kvo)


def whole(shape):
    return pl.BlockSpec(shape, lambda *_: (0,) * len(shape))


def on_device(
    cells,
    is_context,
    labels,
    inducing,
    induce_query,
    column_kvo,
    cell_qkvo,
    class_tokens,
    class_query,
    row_kvo,
    label_table,
    icl_query,
    icl_kvo,
):
    n_src = lax.axis_size("row")
    n_split = lax.axis_size("feat")
    n_rows, n_feat, width = cells.shape
    n_class = class_tokens.shape[0]
    all_rows = n_src * n_rows
    own_feat = n_feat // n_src
    out_rows = n_rows // n_split
    n_ind = inducing.shape[0]
    flags = (is_context == 1).astype(F32)
    window = lax.all_gather(flags, "row", axis=0, tiled=True)
    maskb = jnp.broadcast_to(window.astype(BF16)[:, None], (all_rows, width))

    by_feature = jnp.transpose(cells, (1, 0, 2)).reshape(n_src, own_feat, n_rows, width)
    x = lax.all_to_all(by_feature, "row", split_axis=0, concat_axis=0, tiled=True)
    per_step = 2 if own_feat % 2 == 0 else 1
    weights = (inducing, induce_query, column_kvo, cell_qkvo, class_tokens, class_query, row_kvo)
    sums = pl.pallas_call(
        column_kernel,
        grid=(own_feat // per_step,),
        in_specs=[
            pl.BlockSpec((n_src, per_step, n_rows, width), lambda i: (0, i, 0, 0)),
            whole((all_rows, width)),
        ]
        + [whole(w.shape) for w in weights],
        out_specs=whole((all_rows, (n_class + 1) * width)),
        out_shape=jax.ShapeDtypeStruct((all_rows, (n_class + 1) * width), BF16),
        scratch_shapes=[
            pltpu.VMEM((HEADS * n_ind, width), BF16),
            pltpu.VMEM((n_class * ROW_HEADS, width), BF16),
            pltpu.VMEM((4, width, width), BF16),
            pltpu.VMEM((n_class, width, all_rows), F32),
            pltpu.VMEM((n_class * ROW_HEADS, all_rows), F32),
        ],
        compiler_params=pltpu.CompilerParams(vmem_limit_bytes=48 * 2**20),
    )(x, maskb, *weights)

    n_parts = n_src * n_split
    parts = lax.all_to_all(
        sums.reshape(n_parts, out_rows, -1), ("row", "feat"), split_axis=0, concat_axis=0, tiled=True
    )
    own = lax.dynamic_slice_in_dim(flags, lax.axis_index("feat") * out_rows, out_rows)
    shape = jax.ShapeDtypeStruct((out_rows, n_class * width), BF16)
    row_embed, icl_input = pl.pallas_call(embed_kernel, out_shape=(shape, shape))(
        parts, class_tokens, class_query, row_kvo, own[:, None], labels[:, None], label_table
    )
    inputs = lax.all_gather(icl_input, ("row", "feat"), axis=0, tiled=True)
    return pl.pallas_call(
        context_kernel,
        out_shape=shape,
        compiler_params=pltpu.CompilerParams(vmem_limit_bytes=48 * 2**20),
    )(row_embed, inputs, window[None, :], icl_query, icl_kvo)


def solution(mesh):
    return jax.shard_map(
        on_device,
        mesh=mesh,
        in_specs=(
            P(("group", "row"), "feat", None),
            P(("group", "row")),
            P(("group", "row", "feat")),
            P(),
            P(),
            P(),
            P(),
            P(),
            P(),
            P(),
            P(),
            P(),
            P(),
        ),
        out_specs=P(("group", "row", "feat"), None),
        check_vma=False,
    )
```

```python
import functools
import math

import jax
import jax.numpy as jnp
from jax import lax
from jax.experimental import pallas as pl
from jax.experimental.pallas import tpu as pltpu
from jax.sharding import PartitionSpec as P

HEADS = 4
ROW_HEADS = 8
EPSILON = 1e-06
LOG2E = math.log2(math.e)

F32 = jnp.float32
BF16 = jnp.bfloat16


def mm(a, b):
    return jnp.dot(a, b, preferred_element_type=F32)


def mm_nt(a, b):
    return lax.dot_general(a, b, (((1,), (1,)), ((), ())), preferred_element_type=F32)


def flip(w):
    return w.astype(F32).T.astype(BF16)


def head_rows(shape, row_block, lane_block, n):
    rows = lax.broadcasted_iota(jnp.int32, shape, 0) // row_block
    lanes = lax.broadcasted_iota(jnp.int32, shape, 1) // lane_block
    return lax.rem(rows, n) == lax.rem(lanes, n)


def row_queries(ct, class_query):
    n_class, width = ct.shape
    rq = mm(ct, class_query).astype(BF16).astype(F32)
    shape = (n_class * ROW_HEADS, width)
    rq = jnp.broadcast_to(rq[:, None, :], (n_class, ROW_HEADS, width)).reshape(shape)
    return jnp.where(head_rows(shape, 1, width // ROW_HEADS, ROW_HEADS), rq, 0.0)


def prepare(ind, iq_w, ckvo, cqkvo, ct, cq_w, rkvo, wcol, wrow, wt):
    n_ind, width = ind.shape
    iq = mm(ind[...], iq_w[...]).astype(BF16).astype(F32)
    iq = jnp.concatenate([iq] * HEADS, axis=0)
    iq = jnp.where(head_rows(iq.shape, n_ind, width // HEADS, HEADS), iq, 0.0).astype(BF16)
    scale = LOG2E / math.sqrt(width // HEADS)
    wcol[...] = (mm_nt(iq, ckvo[0]) * scale).astype(BF16)
    rq = row_queries(ct[...], cq_w[...]).astype(BF16)
    row_scale = LOG2E / math.sqrt(width // ROW_HEADS)
    wrow[...] = (mm_nt(rq, rkvo[0]) * row_scale).astype(BF16)
    wt[0] = flip(cqkvo[0])
    wt[1] = flip(cqkvo[2])
    wt[2] = flip(cqkvo[3])
    wt[3] = flip(rkvo[1])


def feature(x, maskb, ind, ckvo, cqkvo, wcol, wrow, wt):
    n_ind, width = ind.shape
    head = width // HEADS
    xt = x.T
    weight = jnp.exp2(mm(wcol[...], xt)).astype(BF16)
    values = mm(x, ckvo[1]).astype(BF16) * maskb
    numer = mm(weight, jnp.concatenate([values, maskb], axis=1))
    ratio = numer[:, :width] / numer[:, width:]
    lane_head = lax.broadcasted_iota(jnp.int32, (n_ind, width), 1) // head
    col_mix = ratio[:n_ind]
    for h in range(1, HEADS):
        col_mix = jnp.where(lane_head == h, ratio[h * n_ind : (h + 1) * n_ind], col_mix)
    summary = (ind[...].astype(F32) + mm(col_mix.astype(BF16), ckvo[2])).astype(BF16)
    scale = LOG2E / math.sqrt(head)
    keys = mm(summary, cqkvo[1]) * scale
    keys = jnp.concatenate([keys] * HEADS, axis=0)
    keys = jnp.where(head_rows(keys.shape, n_ind, head, HEADS), keys, 0.0).astype(BF16)
    sum_values = mm_nt(wt[1], jnp.concatenate([summary] * HEADS, axis=0))
    sum_values = jnp.where(head_rows(sum_values.shape, head, n_ind, HEADS), sum_values, 0.0)
    sum_values = sum_values.astype(BF16)
    query = mm(wt[0], xt).astype(BF16)
    cell = jnp.exp2(mm(keys, query))
    blocks = []
    for h in range(HEADS):
        part = cell[h * n_ind : (h + 1) * n_ind]
        blocks.append((part * (1.0 / jnp.sum(part, axis=0, keepdims=True))).astype(BF16))
    cell = jnp.concatenate(blocks, axis=0)
    mix = mm(sum_values, cell).astype(BF16)
    out = xt.astype(F32) + mm(wt[2], mix)
    inv = lax.rsqrt(jnp.mean(out * out, axis=0, keepdims=True) + EPSILON)
    embedded = (out * inv).astype(BF16)
    row_weight = jnp.exp2(mm(wrow[...], embedded))
    row_values = mm(wt[3], embedded).astype(BF16).astype(F32)
    return row_weight, row_values


def accumulate(terms, acc, den, n_class):
    width = terms[0][1].shape[0]
    total = terms[0][0]
    for weight, _ in terms[1:]:
        total = total + weight
    den[...] += total
    for c in range(n_class):
        add = None
        for weight, values in terms:
            w = weight[c * ROW_HEADS : (c + 1) * ROW_HEADS].astype(BF16).astype(F32)
            n = w.shape[1]
            w = jnp.broadcast_to(w[:, None, :], (ROW_HEADS, width // ROW_HEADS, n)).reshape(width, n)
            add = w * values if add is None else add + w * values
        acc[c] += add


def finish(acc, den, out_ref):
    n_class, width, n_rows = acc.shape
    n_parts, out_rows, _ = out_ref.shape
    for c in range(n_class):
        numer = acc[c].T.astype(BF16).reshape(n_parts, out_rows, width)
        out_ref[:, :, c * width : (c + 1) * width] = numer
    d = den[...]
    pad = jnp.zeros((width - d.shape[0], n_rows), F32)
    d = jnp.concatenate([d, pad], axis=0).T.astype(BF16)
    out_ref[:, :, n_class * width :] = d.reshape(n_parts, out_rows, width)


def embed_rows(total, ct, cq_w, rkvo, context, labels, table):
    n_class, width = ct.shape
    n_rows = total.shape[0]
    queries = row_queries(ct[...], cq_w[...])
    keys = mm(ct[...], rkvo[0]).astype(BF16).astype(F32)
    values = mm(ct[...], rkvo[1]).astype(BF16).astype(F32)
    scale = LOG2E / math.sqrt(width // ROW_HEADS)
    cls_den = jnp.zeros((n_class * ROW_HEADS, 1), F32)
    cls_num = jnp.zeros((n_class * ROW_HEADS, width), F32)
    for t in range(n_class):
        w = jnp.exp2(jnp.sum(queries * keys[t : t + 1], axis=1, keepdims=True) * scale)
        cls_den = cls_den + w
        cls_num = cls_num + w.astype(BF16).astype(F32) * values[t : t + 1]
    shape = cls_num.shape
    own = head_rows(shape, 1, width // ROW_HEADS, ROW_HEADS)
    cls_num = jnp.where(own, cls_num, 0.0)
    cls_den = jnp.where(own, jnp.broadcast_to(cls_den, shape), 0.0)
    lane_head = lax.broadcasted_iota(jnp.int32, (n_rows, width), 1) // (width // ROW_HEADS)
    embeds = []
    for c in range(n_class):
        rows = slice(c * ROW_HEADS, (c + 1) * ROW_HEADS)
        numer = total[:, c * width : (c + 1) * width] + jnp.sum(cls_num[rows], axis=0, keepdims=True)
        denom = jnp.zeros((n_rows, width), F32)
        for h in range(ROW_HEADS):
            at = n_class * width + c * ROW_HEADS + h
            denom = jnp.where(lane_head == h, total[:, at : at + 1], denom)
        denom = denom + jnp.sum(cls_den[rows], axis=0, keepdims=True)
        mix = (numer / denom).astype(BF16)
        embeds.append((ct[c : c + 1].astype(F32) + mm(mix, rkvo[2])).astype(BF16))
    row_embed = jnp.concatenate(embeds, axis=1)
    label_vec = jnp.zeros((n_rows, n_class * width), F32)
    for k in range(table.shape[0]):
        label_vec = jnp.where(labels == k, table[k : k + 1].astype(F32), label_vec)
    icl_input = (row_embed.astype(F32) + context * label_vec).astype(BF16)
    return row_embed, icl_input


def in_context(embed, inputs, mask, icl_q, icl_kvo):
    width = embed.shape[1]
    head = width // HEADS
    query = mm(embed, icl_q[...]).astype(BF16)
    keys = mm(inputs, icl_kvo[0]).astype(BF16)
    values = mm(inputs, icl_kvo[1]).astype(BF16)
    scale = LOG2E / math.sqrt(head)
    mixes = []
    for h in range(HEADS):
        lanes = slice(h * head, (h + 1) * head)
        weight = jnp.exp2(mm_nt(query[:, lanes], keys[:, lanes]) * scale) * mask
        denom = jnp.sum(weight, axis=1, keepdims=True)
        mixes.append((mm(weight.astype(BF16), values[:, lanes]) / denom).astype(BF16))
    mix = jnp.concatenate(mixes, axis=1)
    return (embed.astype(F32) + mm(mix, icl_kvo[2])).astype(BF16)


MESH = pl.DeviceIdType.MESH


def wait_bytes(ref, sem):
    pltpu.make_async_copy(ref, ref, sem).wait()


def window_kernel(
    n_src, n_split, src, mask_src, context, labels, ind, iq_w, ckvo, cqkvo, ct, cq_w, rkvo, table, icl_q, icl_kvo,
    out_ref, xbuf, mbuf, sums, pbuf, own_in, gbuf, wcol, wrow, wt, acc, den,
    x_send, x_recv, x_local, m_send, m_recv, p_send, p_recv, g_send, g_recv, local,
):
    n_chunk, _, per, n_rows, width = xbuf.shape
    n_class = ct.shape[0]
    n_parts, out_rows, _ = pbuf.shape
    all_rows = n_src * n_rows
    me = lax.axis_index("row")
    part = me * n_split + lax.axis_index("feat")

    barrier = pltpu.get_barrier_semaphore()

    def greet(d, carry):
        peer = lax.rem(part + d, n_parts)
        pl.semaphore_signal(
            barrier, inc=1, device_id={"row": peer // n_split, "feat": lax.rem(peer, n_split)}, device_id_type=MESH
        )
        return carry

    lax.fori_loop(1, n_parts, greet, 0)
    pl.semaphore_wait(barrier, n_parts - 1)

    def send_mask(d, carry):
        peer = lax.rem(me + d, n_src)
        pltpu.make_async_remote_copy(
            src_ref=mask_src, dst_ref=mbuf.at[me], send_sem=m_send, recv_sem=m_recv,
            device_id={"row": peer}, device_id_type=MESH,
        ).start()
        return carry

    lax.fori_loop(1, n_src, send_mask, 0)

    def send_chunk(k, carry):
        def send(d, inner):
            peer = lax.rem(me + d, n_src)
            pltpu.make_async_remote_copy(
                src_ref=src.at[peer, k], dst_ref=xbuf.at[k, me], send_sem=x_send.at[k], recv_sem=x_recv.at[k],
                device_id={"row": peer}, device_id_type=MESH,
            ).start()
            return inner

        lax.fori_loop(1, n_src, send, 0)
        pltpu.make_async_copy(src.at[me, k], xbuf.at[k, me], x_local.at[k]).start()
        return carry

    lax.fori_loop(0, n_chunk, send_chunk, 0)
    own_mask = pltpu.make_async_copy(mask_src, mbuf.at[me], local.at[0])
    own_mask.start()

    prepare(ind, iq_w, ckvo, cqkvo, ct, cq_w, rkvo, wcol, wrow, wt)
    acc[...] = jnp.zeros_like(acc)
    den[...] = jnp.zeros_like(den)
    wait_bytes(mbuf.at[pl.ds(0, n_src - 1)], m_recv)
    own_mask.wait()

    def work(k, carry):
        wait_bytes(xbuf.at[k, pl.ds(0, n_src - 1)], x_recv.at[k])
        pltpu.make_async_copy(src.at[me, k], xbuf.at[k, me], x_local.at[k]).wait()
        maskb = mbuf[...].reshape(all_rows, width)
        terms = []
        for f in range(per):
            x = xbuf[k, :, f].reshape(all_rows, width)
            terms.append(feature(x, maskb, ind, ckvo, cqkvo, wcol, wrow, wt))
        accumulate(terms, acc, den, n_class)
        return carry

    lax.fori_loop(0, n_chunk, work, 0)
    finish(acc, den, sums)

    def exchange(make):
        def send(d, carry):
            peer = lax.rem(part + d, n_parts)
            make(peer, {"row": peer // n_split, "feat": lax.rem(peer, n_split)}).start()
            return carry

        lax.fori_loop(1, n_parts, send, 0)

    exchange(
        lambda peer, device: pltpu.make_async_remote_copy(
            src_ref=sums.at[peer], dst_ref=pbuf.at[part], send_sem=p_send, recv_sem=p_recv,
            device_id=device, device_id_type=MESH,
        )
    )
    own_sums = pltpu.make_async_copy(sums.at[part], pbuf.at[part], local.at[1])
    own_sums.start()
    mask = jnp.transpose(mbuf[...].reshape(all_rows, width).astype(F32))[:1]
    own_sums.wait()
    wait_bytes(pbuf.at[pl.ds(0, n_parts - 1)], p_recv)
    total = jnp.sum(pbuf[...].astype(F32), axis=0)
    embed, inputs = embed_rows(total, ct, cq_w, rkvo, context[...], labels[...], table)
    own_in[...] = inputs
    exchange(
        lambda peer, device: pltpu.make_async_remote_copy(
            src_ref=own_in, dst_ref=gbuf.at[part], send_sem=g_send, recv_sem=g_recv,
            device_id=device, device_id_type=MESH,
        )
    )
    own_inputs = pltpu.make_async_copy(own_in, gbuf.at[part], local.at[2])
    own_inputs.start()
    own_inputs.wait()
    wait_bytes(gbuf.at[pl.ds(0, n_parts - 1)], g_recv)
    window = gbuf[...].reshape(all_rows, n_class * width)
    out_ref[...] = in_context(embed, window, mask, icl_q, icl_kvo)

    wait_bytes(mbuf.at[pl.ds(0, n_src - 1)], m_send)

    def sent(k, carry):
        wait_bytes(xbuf.at[k, pl.ds(0, n_src - 1)], x_send.at[k])
        return carry

    lax.fori_loop(0, n_chunk, sent, 0)
    wait_bytes(pbuf.at[pl.ds(0, n_parts - 1)], p_send)
    wait_bytes(gbuf.at[pl.ds(0, n_parts - 1)], g_send)


def on_device(
    cells,
    is_context,
    labels,
    inducing,
    induce_query,
    column_kvo,
    cell_qkvo,
    class_tokens,
    class_query,
    row_kvo,
    label_table,
    icl_query,
    icl_kvo,
):
    n_src = lax.axis_size("row")
    n_split = lax.axis_size("feat")
    n_rows, n_feat, width = cells.shape
    n_class = class_tokens.shape[0]
    all_rows = n_src * n_rows
    own_feat = n_feat // n_src
    out_rows = n_rows // n_split
    n_ind = inducing.shape[0]
    n_parts = n_src * n_split
    per_chunk = 2 if own_feat % 2 == 0 else 1
    n_chunk = own_feat // per_chunk
    d3 = n_class * width
    flags = (is_context == 1).astype(F32)
    mask = jnp.broadcast_to(flags.astype(BF16)[:, None], (n_rows, width))
    by_feature = jnp.transpose(cells, (1, 0, 2)).reshape(n_src, n_chunk, per_chunk, n_rows, width)
    own = lax.dynamic_slice_in_dim(flags, lax.axis_index("feat") * out_rows, out_rows)
    vmem = pl.BlockSpec(memory_space=pltpu.VMEM)
    dma = pltpu.SemaphoreType.DMA
    return pl.pallas_call(
        functools.partial(window_kernel, n_src, n_split),
        in_specs=[pl.BlockSpec(memory_space=pl.ANY)] + [vmem] * 13,
        out_specs=vmem,
        out_shape=jax.ShapeDtypeStruct((out_rows, d3), BF16),
        scratch_shapes=[
            pltpu.VMEM((n_chunk, n_src, per_chunk, n_rows, width), BF16),
            pltpu.VMEM((n_src, n_rows, width), BF16),
            pltpu.VMEM((n_parts, out_rows, d3 + width), BF16),
            pltpu.VMEM((n_parts, out_rows, d3 + width), BF16),
            pltpu.VMEM((out_rows, d3), BF16),
            pltpu.VMEM((n_parts, out_rows, d3), BF16),
            pltpu.VMEM((HEADS * n_ind, width), BF16),
            pltpu.VMEM((n_class * ROW_HEADS, width), BF16),
            pltpu.VMEM((4, width, width), BF16),
            pltpu.VMEM((n_class, width, all_rows), F32),
            pltpu.VMEM((n_class * ROW_HEADS, all_rows), F32),
            dma((n_chunk,)),
            dma((n_chunk,)),
            dma((n_chunk,)),
            dma,
            dma,
            dma,
            dma,
            dma,
            dma,
            dma((3,)),
        ],
        compiler_params=pltpu.CompilerParams(
            vmem_limit_bytes=48 * 2**20, collective_id=0, has_side_effects=True
        ),
    )(
        by_feature,
        mask,
        own[:, None],
        labels[:, None],
        inducing,
        induce_query,
        column_kvo,
        cell_qkvo,
        class_tokens,
        class_query,
        row_kvo,
        label_table,
        icl_query,
        icl_kvo,
    )


def solution(mesh):
    return jax.shard_map(
        on_device,
        mesh=mesh,
        in_specs=(
            P(("group", "row"), "feat", None),
            P(("group", "row")),
            P(("group", "row", "feat")),
            P(),
            P(),
            P(),
            P(),
            P(),
            P(),
            P(),
            P(),
            P(),
            P(),
        ),
        out_specs=P(("group", "row", "feat"), None),
        check_vma=False,
    )
```

```python
import functools
import math

import jax
import jax.numpy as jnp
from jax import lax
from jax.experimental import pallas as pl
from jax.experimental.pallas import tpu as pltpu
from jax.sharding import PartitionSpec as P

HEADS = 4
ROW_HEADS = 8
EPSILON = 1e-06
LOG2E = math.log2(math.e)

F32 = jnp.float32
BF16 = jnp.bfloat16


def mm(a, b):
    return jnp.dot(a, b, preferred_element_type=F32)


def mm_nt(a, b):
    return lax.dot_general(a, b, (((1,), (1,)), ((), ())), preferred_element_type=F32)


def flip(w):
    return w.astype(F32).T.astype(BF16)


def head_rows(shape, row_block, lane_block, n):
    rows = lax.broadcasted_iota(jnp.int32, shape, 0) // row_block
    lanes = lax.broadcasted_iota(jnp.int32, shape, 1) // lane_block
    return lax.rem(rows, n) == lax.rem(lanes, n)


def row_queries(ct, class_query):
    n_class, width = ct.shape
    rq = mm(ct, class_query).astype(BF16).astype(F32)
    shape = (n_class * ROW_HEADS, width)
    rq = jnp.broadcast_to(rq[:, None, :], (n_class, ROW_HEADS, width)).reshape(shape)
    return jnp.where(head_rows(shape, 1, width // ROW_HEADS, ROW_HEADS), rq, 0.0)


def prepare(ind, iq_w, ckvo, cqkvo, ct, cq_w, rkvo, wcol, wrow, wt):
    n_ind, width = ind.shape
    iq = mm(ind[...], iq_w[...]).astype(BF16).astype(F32)
    iq = jnp.concatenate([iq] * HEADS, axis=0)
    iq = jnp.where(head_rows(iq.shape, n_ind, width // HEADS, HEADS), iq, 0.0).astype(BF16)
    scale = LOG2E / math.sqrt(width // HEADS)
    wcol[...] = (mm_nt(iq, ckvo[0]) * scale).astype(BF16)
    rq = row_queries(ct[...], cq_w[...]).astype(BF16)
    row_scale = LOG2E / math.sqrt(width // ROW_HEADS)
    wrow[...] = (mm_nt(rq, rkvo[0]) * row_scale).astype(BF16)
    wt[0] = flip(cqkvo[0])
    wt[1] = flip(cqkvo[2])
    wt[2] = flip(cqkvo[3])
    wt[3] = flip(rkvo[1])


def feature(x, maskb, ind, ckvo, cqkvo, wcol, wrow, wt):
    n_ind, width = ind.shape
    head = width // HEADS
    xt = x.T
    weight = jnp.exp2(mm(wcol[...], xt)).astype(BF16)
    values = mm(x, ckvo[1]).astype(BF16) * maskb
    numer = mm(weight, jnp.concatenate([values, maskb], axis=1))
    ratio = numer[:, :width] / numer[:, width:]
    lane_head = lax.broadcasted_iota(jnp.int32, (n_ind, width), 1) // head
    col_mix = ratio[:n_ind]
    for h in range(1, HEADS):
        col_mix = jnp.where(lane_head == h, ratio[h * n_ind : (h + 1) * n_ind], col_mix)
    summary = (ind[...].astype(F32) + mm(col_mix.astype(BF16), ckvo[2])).astype(BF16)
    scale = LOG2E / math.sqrt(head)
    keys = mm(summary, cqkvo[1]) * scale
    keys = jnp.concatenate([keys] * HEADS, axis=0)
    keys = jnp.where(head_rows(keys.shape, n_ind, head, HEADS), keys, 0.0).astype(BF16)
    sum_values = mm_nt(wt[1], jnp.concatenate([summary] * HEADS, axis=0))
    sum_values = jnp.where(head_rows(sum_values.shape, head, n_ind, HEADS), sum_values, 0.0)
    sum_values = sum_values.astype(BF16)
    query = mm(wt[0], xt).astype(BF16)
    cell = jnp.exp2(mm(keys, query))
    blocks = []
    for h in range(HEADS):
        part = cell[h * n_ind : (h + 1) * n_ind]
        blocks.append((part * (1.0 / jnp.sum(part, axis=0, keepdims=True))).astype(BF16))
    cell = jnp.concatenate(blocks, axis=0)
    mix = mm(sum_values, cell).astype(BF16)
    out = xt.astype(F32) + mm(wt[2], mix)
    inv = lax.rsqrt(jnp.mean(out * out, axis=0, keepdims=True) + EPSILON)
    embedded = (out * inv).astype(BF16)
    row_weight = jnp.exp2(mm(wrow[...], embedded))
    row_values = mm(wt[3], embedded).astype(BF16).astype(F32)
    return row_weight, row_values


def accumulate(terms, acc, den, n_class):
    width = terms[0][1].shape[0]
    total = terms[0][0]
    for weight, _ in terms[1:]:
        total = total + weight
    den[...] += total
    for c in range(n_class):
        add = None
        for weight, values in terms:
            w = weight[c * ROW_HEADS : (c + 1) * ROW_HEADS].astype(BF16).astype(F32)
            n = w.shape[1]
            w = jnp.broadcast_to(w[:, None, :], (ROW_HEADS, width // ROW_HEADS, n)).reshape(width, n)
            add = w * values if add is None else add + w * values
        acc[c] += add


def finish(acc, den, out_ref):
    n_class, width, n_rows = acc.shape
    _, _, n_outer, out_rows, _ = out_ref.shape
    d = den[...]
    pad = jnp.zeros((width - d.shape[0], n_rows), F32)
    pieces = [acc[c] for c in range(n_class)] + [jnp.concatenate([d, pad], axis=0)]
    for i, piece in enumerate(pieces):
        rows = piece.T.astype(BF16).reshape(n_outer, 2, 2, out_rows, width)
        for b in range(2):
            for c in range(2):
                out_ref[c, b, :, :, i * width : (i + 1) * width] = rows[:, b, c]


def column(row, first, n):
    shape = (n, row.shape[1])
    wanted = lax.broadcasted_iota(jnp.int32, shape, 0) + first
    here = lax.broadcasted_iota(jnp.int32, shape, 1) == wanted
    return jnp.sum(jnp.where(here, jnp.broadcast_to(row, shape), 0.0), axis=1, keepdims=True)


def embed_rows(total, ct, cq_w, rkvo, context, labels, table):
    n_class, width = ct.shape
    n_rows = total.shape[0]
    queries = row_queries(ct[...], cq_w[...])
    keys = mm(ct[...], rkvo[0]).astype(BF16).astype(F32)
    values = mm(ct[...], rkvo[1]).astype(BF16).astype(F32)
    scale = LOG2E / math.sqrt(width // ROW_HEADS)
    cls_den = jnp.zeros((n_class * ROW_HEADS, 1), F32)
    cls_num = jnp.zeros((n_class * ROW_HEADS, width), F32)
    for t in range(n_class):
        w = jnp.exp2(jnp.sum(queries * keys[t : t + 1], axis=1, keepdims=True) * scale)
        cls_den = cls_den + w
        cls_num = cls_num + w.astype(BF16).astype(F32) * values[t : t + 1]
    shape = cls_num.shape
    own = head_rows(shape, 1, width // ROW_HEADS, ROW_HEADS)
    cls_num = jnp.where(own, cls_num, 0.0)
    cls_den = jnp.where(own, jnp.broadcast_to(cls_den, shape), 0.0)
    lane_head = lax.broadcasted_iota(jnp.int32, (n_rows, width), 1) // (width // ROW_HEADS)
    embeds = []
    for c in range(n_class):
        rows = slice(c * ROW_HEADS, (c + 1) * ROW_HEADS)
        numer = total[:, c * width : (c + 1) * width] + jnp.sum(cls_num[rows], axis=0, keepdims=True)
        denom = jnp.zeros((n_rows, width), F32)
        for h in range(ROW_HEADS):
            at = n_class * width + c * ROW_HEADS + h
            denom = jnp.where(lane_head == h, total[:, at : at + 1], denom)
        denom = denom + jnp.sum(cls_den[rows], axis=0, keepdims=True)
        mix = (numer / denom).astype(BF16)
        embeds.append((ct[c : c + 1].astype(F32) + mm(mix, rkvo[2])).astype(BF16))
    row_embed = jnp.concatenate(embeds, axis=1)
    label_vec = jnp.zeros((n_rows, n_class * width), F32)
    for k in range(table.shape[0]):
        label_vec = jnp.where(labels == k, table[k : k + 1].astype(F32), label_vec)
    icl_input = (row_embed.astype(F32) + context * label_vec).astype(BF16)
    return row_embed, icl_input


def in_context(embed, inputs, mask, icl_q, icl_kvo):
    width = embed.shape[1]
    head = width // HEADS
    query = mm(embed, icl_q[...]).astype(BF16)
    keys = mm(inputs, icl_kvo[0]).astype(BF16)
    values = mm(inputs, icl_kvo[1]).astype(BF16)
    scale = LOG2E / math.sqrt(head)
    mixes = []
    for h in range(HEADS):
        lanes = slice(h * head, (h + 1) * head)
        weight = jnp.exp2(mm_nt(query[:, lanes], keys[:, lanes]) * scale) * mask
        denom = jnp.sum(weight, axis=1, keepdims=True)
        mixes.append((mm(weight.astype(BF16), values[:, lanes]) / denom).astype(BF16))
    mix = jnp.concatenate(mixes, axis=1)
    return (embed.astype(F32) + mm(mix, icl_kvo[2])).astype(BF16)


MESH = pl.DeviceIdType.MESH


def wait_bytes(ref, sem):
    pltpu.make_async_copy(ref, ref, sem).wait()


def window_kernel(
    n_src, n_split, src, context, labels, ind, iq_w, ckvo, cqkvo, ct, cq_w, rkvo, table, icl_q, icl_kvo,
    out_ref, xbuf, mask_src, mbuf, sums, core_in, core_sum, near_in, near_sum, pbuf, gbuf, wcol, wrow, wt, acc, den,
    x_send, x_recv, x_local, m_send, m_recv, pair_send, pair_recv, p_send, p_recv, g_send, g_recv, far_recv, local,
):
    n_chunk, _, per, n_rows, width = xbuf.shape
    n_class = ct.shape[0]
    n_outer, out_rows, _ = pbuf.shape
    n_parts = n_outer * 4
    all_rows = n_src * n_rows
    me = lax.axis_index("row")
    part = me * n_split + lax.axis_index("feat")

    outer, inner = part // 4, lax.rem(part, 4)
    flags = jnp.where(context[...] == 1, 1.0, 0.0)
    mask_src[...] = jnp.broadcast_to(column(flags, 0, n_rows), mask_src.shape).astype(BF16)

    def device(p):
        return {"row": p // n_split, "feat": lax.rem(p, n_split)}

    barrier = pltpu.get_barrier_semaphore()

    def greet(d, carry):
        peer = lax.rem(part + d, n_parts)
        pl.semaphore_signal(
            barrier, inc=1, device_id=device(peer), device_id_type=MESH
        )
        return carry

    lax.fori_loop(1, n_parts, greet, 0)
    pl.semaphore_wait(barrier, n_parts - 1)

    def send_mask(d, carry):
        peer = lax.rem(me + d, n_src)
        pltpu.make_async_remote_copy(
            src_ref=mask_src, dst_ref=mbuf.at[me], send_sem=m_send, recv_sem=m_recv,
            device_id={"row": peer}, device_id_type=MESH,
        ).start()
        return carry

    lax.fori_loop(1, n_src, send_mask, 0)

    def send_chunk(k, carry):
        def send(d, inner):
            peer = lax.rem(me + d, n_src)
            pltpu.make_async_remote_copy(
                src_ref=src.at[peer, k], dst_ref=xbuf.at[k, me], send_sem=x_send.at[k], recv_sem=x_recv.at[k],
                device_id={"row": peer}, device_id_type=MESH,
            ).start()
            return inner

        lax.fori_loop(1, n_src, send, 0)
        pltpu.make_async_copy(src.at[me, k], xbuf.at[k, me], x_local.at[k]).start()
        return carry

    lax.fori_loop(0, n_chunk, send_chunk, 0)
    own_mask = pltpu.make_async_copy(mask_src, mbuf.at[me], local.at[0])
    own_mask.start()

    prepare(ind, iq_w, ckvo, cqkvo, ct, cq_w, rkvo, wcol, wrow, wt)
    acc[...] = jnp.zeros_like(acc)
    den[...] = jnp.zeros_like(den)
    wait_bytes(mbuf.at[pl.ds(0, n_src - 1)], m_recv)
    own_mask.wait()

    def work(k, carry):
        wait_bytes(xbuf.at[k, pl.ds(0, n_src - 1)], x_recv.at[k])
        pltpu.make_async_copy(src.at[me, k], xbuf.at[k, me], x_local.at[k]).wait()
        maskb = mbuf[...].reshape(all_rows, width)
        terms = []
        for f in range(per):
            x = xbuf[k, :, f].reshape(all_rows, width)
            terms.append(feature(x, maskb, ind, ckvo, cqkvo, wcol, wrow, wt))
        accumulate(terms, acc, den, n_class)
        return carry

    lax.fori_loop(0, n_chunk, work, 0)
    finish(acc, den, sums)

    own_core, own_near = lax.rem(inner, 2), inner // 2
    pair = pltpu.make_async_remote_copy(
        src_ref=sums.at[1 - own_core], dst_ref=core_in, send_sem=pair_send.at[0], recv_sem=pair_recv.at[0],
        device_id=device(part + 1 - 2 * own_core), device_id_type=MESH,
    )
    pair.start()
    mask = jnp.transpose(mbuf[...].reshape(all_rows, width).astype(F32))[:1]
    pair.wait()
    core_sum[...] = (sums[own_core].astype(F32) + core_in[...].astype(F32)).astype(BF16)
    pair = pltpu.make_async_remote_copy(
        src_ref=core_sum.at[1 - own_near], dst_ref=near_in, send_sem=pair_send.at[1], recv_sem=pair_recv.at[1],
        device_id=device(part + 2 - 4 * own_near), device_id_type=MESH,
    )
    pair.start()
    pair.wait()
    near_sum[...] = (core_sum[own_near].astype(F32) + near_in[...].astype(F32)).astype(BF16)

    def send_sums(d, carry):
        peer = lax.rem(outer + d, n_outer)
        pltpu.make_async_remote_copy(
            src_ref=near_sum.at[peer], dst_ref=pbuf.at[outer], send_sem=p_send, recv_sem=p_recv,
            device_id=device(peer * 4 + inner), device_id_type=MESH,
        ).start()
        return carry

    lax.fori_loop(1, n_outer, send_sums, 0)
    pbuf[outer] = near_sum[outer]
    wait_bytes(pbuf.at[pl.ds(0, n_outer - 1)], p_recv)
    total = jnp.sum(pbuf[...].astype(F32), axis=0)
    own_flags = column(flags, lax.axis_index("feat") * out_rows, out_rows)
    own_labels = column(labels[...].astype(F32), 0, out_rows).astype(jnp.int32)
    embed, inputs = embed_rows(total, ct, cq_w, rkvo, own_flags, own_labels, table)
    gbuf[part] = inputs

    def send_far(d, carry):
        peer = lax.rem(outer + d, n_outer)
        pltpu.make_async_remote_copy(
            src_ref=gbuf.at[part], dst_ref=gbuf.at[part], send_sem=g_send, recv_sem=far_recv.at[outer],
            device_id=device(peer * 4 + inner), device_id_type=MESH,
        ).start()
        return carry

    lax.fori_loop(1, n_outer, send_far, 0)

    def send_near(slot):
        for d in range(1, 4):
            pltpu.make_async_remote_copy(
                src_ref=gbuf.at[slot], dst_ref=gbuf.at[slot], send_sem=g_send, recv_sem=g_recv,
                device_id=device(outer * 4 + lax.rem(inner + d, 4)), device_id_type=MESH,
            ).start()

    send_near(part)

    def forward(d, carry):
        peer = lax.rem(outer + d, n_outer)
        wait_bytes(gbuf.at[peer * 4 + inner], far_recv.at[peer])
        send_near(peer * 4 + inner)
        return carry

    lax.fori_loop(1, n_outer, forward, 0)
    wait_bytes(gbuf.at[pl.ds(0, 3 * n_outer)], g_recv)
    window = gbuf[...].reshape(all_rows, n_class * width)
    out_ref[...] = in_context(embed, window, mask, icl_q, icl_kvo)

    wait_bytes(mbuf.at[pl.ds(0, n_src - 1)], m_send)

    def sent(k, carry):
        wait_bytes(xbuf.at[k, pl.ds(0, n_src - 1)], x_send.at[k])
        return carry

    lax.fori_loop(0, n_chunk, sent, 0)
    wait_bytes(pbuf.at[pl.ds(0, n_outer - 1)], p_send)
    wait_bytes(gbuf.at[pl.ds(0, n_parts - 1)], g_send)


def on_device(
    cells,
    is_context,
    labels,
    inducing,
    induce_query,
    column_kvo,
    cell_qkvo,
    class_tokens,
    class_query,
    row_kvo,
    label_table,
    icl_query,
    icl_kvo,
):
    n_src = lax.axis_size("row")
    n_split = lax.axis_size("feat")
    n_rows, n_feat, width = cells.shape
    n_class = class_tokens.shape[0]
    all_rows = n_src * n_rows
    own_feat = n_feat // n_src
    out_rows = n_rows // n_split
    n_ind = inducing.shape[0]
    n_parts = n_src * n_split
    per_chunk = 2 if own_feat % 2 == 0 else 1
    n_chunk = own_feat // per_chunk
    d3 = n_class * width
    n_outer = n_parts // 4
    by_feature = jnp.transpose(cells, (1, 0, 2)).reshape(n_src, n_chunk, per_chunk, n_rows, width)
    vmem = pl.BlockSpec(memory_space=pltpu.VMEM)
    dma = pltpu.SemaphoreType.DMA
    return pl.pallas_call(
        functools.partial(window_kernel, n_src, n_split),
        in_specs=[pl.BlockSpec(memory_space=pl.ANY)] + [vmem] * 12,
        out_specs=vmem,
        out_shape=jax.ShapeDtypeStruct((out_rows, d3), BF16),
        scratch_shapes=[
            pltpu.VMEM((n_chunk, n_src, per_chunk, n_rows, width), BF16),
            pltpu.VMEM((n_rows, width), BF16),
            pltpu.VMEM((n_src, n_rows, width), BF16),
            pltpu.VMEM((2, 2, n_outer, out_rows, d3 + width), BF16),
            pltpu.VMEM((2, n_outer, out_rows, d3 + width), BF16),
            pltpu.VMEM((2, n_outer, out_rows, d3 + width), BF16),
            pltpu.VMEM((n_outer, out_rows, d3 + width), BF16),
            pltpu.VMEM((n_outer, out_rows, d3 + width), BF16),
            pltpu.VMEM((n_outer, out_rows, d3 + width), BF16),
            pltpu.VMEM((n_parts, out_rows, d3), BF16),
            pltpu.VMEM((HEADS * n_ind, width), BF16),
            pltpu.VMEM((n_class * ROW_HEADS, width), BF16),
            pltpu.VMEM((4, width, width), BF16),
            pltpu.VMEM((n_class, width, all_rows), F32),
            pltpu.VMEM((n_class * ROW_HEADS, all_rows), F32),
            dma((n_chunk,)),
            dma((n_chunk,)),
            dma((n_chunk,)),
            dma,
            dma,
            dma((2,)),
            dma((2,)),
            dma,
            dma,
            dma,
            dma,
            dma((n_outer,)),
            dma((1,)),
        ],
        compiler_params=pltpu.CompilerParams(
            vmem_limit_bytes=48 * 2**20, collective_id=0, has_side_effects=True
        ),
    )(
        by_feature,
        is_context[None, :],
        labels[None, :],
        inducing,
        induce_query,
        column_kvo,
        cell_qkvo,
        class_tokens,
        class_query,
        row_kvo,
        label_table,
        icl_query,
        icl_kvo,
    )


def solution(mesh):
    return jax.shard_map(
        on_device,
        mesh=mesh,
        in_specs=(
            P(("group", "row"), "feat", None),
            P(("group", "row")),
            P(("group", "row", "feat")),
            P(),
            P(),
            P(),
            P(),
            P(),
            P(),
            P(),
            P(),
            P(),
            P(),
        ),
        out_specs=P(("group", "row", "feat"), None),
        check_vma=False,
    )
```
